32 devices in a mesh: seq: 2 (over x), fsdp: 16 (over z, y, core).
Axes of the slice: x: 2, y: 2, z: 4, core: 2. Of those that a mesh axis runs over, the one named last changes fastest.
Arguments:
- signal: bfloat16 [16, 64, 20, 256], P('fsdp', None, 'seq'), may hold values from -20 to 20
- conv_weight: bfloat16 [256, 2048], P(None, 'fsdp')
- conv_bias: bfloat16 [2048], P('fsdp'), may hold values from -3 to 3
- ln_gain: bfloat16 [2048], P('fsdp'), may hold values from 0.099609375 to 1.8984375
- ln_bias: bfloat16 [2048], P('fsdp'), may hold values from -3 to 3
- w_space: bfloat16 [1024, 3072], P('fsdp')
- w_time: bfloat16 [1024, 3072], P('fsdp')
- w_out: bfloat16 [2048, 2048], P('fsdp'), may hold values from -0.125 to 0.125
Outputs:
- mixed: bfloat16 [16, 64, 20, 2048], P('fsdp', None, 'seq')
The draws below stay inside these ranges and needn't reach their ends.
All inputs are finite; a program needn't handle non-finite values.
Results may differ from the reference program's by a relative error of at most 0.0054.
Values may be sent and summed in bfloat16 or wider, within the bound.
A program may use at most 128 MiB of HBM per device.

```python
import math
import jax
import jax.numpy as jnp
from jax import lax

D = 2048
HEADS = 16
CH = 64
KS = 256
PATCHES = 20
NIGHTS = 16


def draw_signal(key, part):
    key = jax.random.fold_in(key, 13)
    keys = jax.random.split(key, 2)
    shape = (NIGHTS, CH, PATCHES, KS)
    base = jnp.clip(jax.random.normal(keys[0], shape, jnp.float32), -6.0, 6.0)
    level = jnp.exp(jax.random.uniform(keys[1], (NIGHTS, CH, PATCHES, 1), jnp.float32, math.log(0.3), math.log(3.0)))
    values = base * level
    return values.astype(jnp.bfloat16)


def draw_conv_weight(key, part):
    key = jax.random.fold_in(key, 14)
    keys = jax.random.split(key, 2)
    base = jnp.clip(jax.random.normal(keys[0], (KS, D), jnp.float32), -6.0, 6.0)
    column_scale = jnp.exp(jax.random.uniform(keys[1], (1, D), jnp.float32, math.log(0.3), math.log(3.0)))
    return (base * column_scale / math.sqrt(KS)).astype(jnp.bfloat16)


def projection(key):
    in_rows = D // 2
    keys = jax.random.split(key, 1)
    whole = jnp.clip(jax.random.normal(keys[0], (in_rows, 3 * in_rows), jnp.float32), -6.0, 6.0) / math.sqrt(in_rows)
    return whole.astype(jnp.bfloat16)


def draw_w_space(key, part):
    return projection(jax.random.fold_in(key, 11))


def draw_w_time(key, part):
    return projection(jax.random.fold_in(key, 12))


def block_scale(rng, dims, cuts, least, top_value):
    loudness = 1.0
    for dim, shards_of in cuts:
        steps = jax.random.uniform(jax.random.fold_in(jax.random.fold_in(rng, 6), dim), (shards_of,), jnp.float32, least / len(cuts), top_value / len(cuts))
        loudness = loudness * jnp.repeat(jnp.exp(steps), dims[dim] // shards_of).reshape((-1,) + (1,) * (len(dims) - 1 - dim))
    return loudness


def gaussian(stream_key, shape, deviation, bound, cuts=(), dtype=jnp.bfloat16):
    level = block_scale(stream_key, shape, cuts, -0.22, 0.18) if cuts else 1.0
    drawn = jax.random.normal(stream_key, shape, jnp.float32) * deviation * level
    return jnp.minimum(jnp.maximum(drawn, -bound), bound).astype(dtype)


def setup_inputs(seed: int = 0) -> dict:
    key_of = jax.random.split(jax.random.key(seed), 9)
    return {
        "signal": draw_signal(jax.random.fold_in(key_of[8], 71), 0),
        "conv_weight": draw_conv_weight(jax.random.fold_in(key_of[8], 71), 0),
        "conv_bias": gaussian(key_of[2], (D,), 0.5, 3.0, ((0, 16),)),
        "ln_gain": jnp.clip(1.0 + 0.18 * jax.random.normal(key_of[3], (D,), jnp.float32), 0.099609375, 1.8984375).astype(jnp.bfloat16),
        "ln_bias": gaussian(key_of[4], (D,), 0.3, 3.0, ((0, 16),)),
        "w_space": draw_w_space(jax.random.fold_in(key_of[8], 71), 0),
        "w_time": draw_w_time(jax.random.fold_in(key_of[8], 71), 0),
        "w_out": gaussian(key_of[7], (D, D), D ** -0.5, 0.125, ((0, 16),)),
    }


def layer_norm(values, gain, shift):
    mean = lax.optimization_barrier(jnp.mean(values, axis=-1, keepdims=True))
    centred = values - mean
    variance = lax.optimization_barrier(jnp.mean(centred * centred, axis=-1, keepdims=True))
    return centred * lax.rsqrt(variance + 1e-05) * gain.astype(jnp.float32) + shift.astype(jnp.float32)

def attend(queries, keys_in, values_in):
    scale = 1.0 / math.sqrt(queries.shape[-1])
    scores = jnp.einsum('bqhd,bkhd->bhqk', queries.astype(jnp.float32), keys_in.astype(jnp.float32)) * scale
    highest = lax.optimization_barrier(jnp.max(scores, axis=-1, keepdims=True))
    expo = jnp.exp(scores - highest)
    probs = (expo / lax.optimization_barrier(jnp.sum(expo, axis=-1, keepdims=True))).astype(jnp.bfloat16)
    probs = lax.optimization_barrier(probs)
    result = jnp.einsum('bhqk,bkhd->bqhd', probs.astype(jnp.float32), values_in.astype(jnp.float32))
    return lax.optimization_barrier(result.astype(jnp.bfloat16))

def reference(signal, conv_weight, conv_bias, ln_gain, ln_bias, w_space, w_time, w_out):
    half_width = D // 2
    head_count = HEADS // 2
    head_size = D // HEADS

    def one_night(night):
        flat = night.reshape(-1, KS)
        embed = (jnp.dot(flat, conv_weight, preferred_element_type=jnp.float32) + conv_bias.astype(jnp.float32)).astype(jnp.bfloat16)
        embed = lax.optimization_barrier(embed)
        normed = layer_norm(embed.astype(jnp.float32), ln_gain, ln_bias).astype(jnp.bfloat16)
        normed = lax.optimization_barrier(normed)
        space_qkv = jnp.dot(normed[:, :half_width], w_space, preferred_element_type=jnp.float32).astype(jnp.bfloat16)
        space_qkv = lax.optimization_barrier(space_qkv)
        space_qkv = space_qkv.reshape(CH, PATCHES, 3, head_count, head_size).transpose(1, 0, 2, 3, 4)
        space_out = attend(space_qkv[:, :, 0], space_qkv[:, :, 1], space_qkv[:, :, 2])
        space_out = space_out.transpose(1, 0, 2, 3).reshape(-1, half_width)
        time_qkv = jnp.dot(normed[:, half_width:], w_time, preferred_element_type=jnp.float32).astype(jnp.bfloat16)
        time_qkv = lax.optimization_barrier(time_qkv)
        time_qkv = time_qkv.reshape(CH, PATCHES, 3, head_count, head_size)
        time_out = attend(time_qkv[:, :, 0], time_qkv[:, :, 1], time_qkv[:, :, 2]).reshape(-1, half_width)
        joined = jnp.concatenate([space_out, time_out], axis=1)
        mixed = embed.astype(jnp.float32) + jnp.dot(joined, w_out, preferred_element_type=jnp.float32)
        return mixed.astype(jnp.bfloat16).reshape(CH, PATCHES, D)
    return lax.map(one_night, signal)
```

```python
import math

import jax
import jax.numpy as jnp
from jax import lax
from jax.experimental import pallas as pl
from jax.experimental.pallas import tpu as pltpu
from jax.sharding import PartitionSpec as P

HEADS = 16
MESH = pl.DeviceIdType.MESH


def layer_norm(values, gain, shift):
    mean = jnp.mean(values, axis=-1, keepdims=True)
    centred = values - mean
    variance = jnp.mean(centred * centred, axis=-1, keepdims=True)
    return centred * lax.rsqrt(variance + 1e-05) * gain.astype(jnp.float32) + shift.astype(
        jnp.float32
    )


def attend(queries, keys_in, values_in):
    scale = 1.0 / math.sqrt(queries.shape[-1])
    scores = (
        jnp.einsum("bqhd,bkhd->bhqk", queries, keys_in, preferred_element_type=jnp.float32) * scale
    )
    highest = jnp.max(scores, axis=-1, keepdims=True)
    expo = jnp.exp(scores - highest)
    probs = (expo / jnp.sum(expo, axis=-1, keepdims=True)).astype(jnp.bfloat16)
    result = jnp.einsum("bhqk,bkhd->bqhd", probs, values_in, preferred_element_type=jnp.float32)
    return result.astype(jnp.bfloat16)


def project(features, weight):
    return jnp.dot(
        features,
        lax.all_gather(weight, "fsdp", axis=0, tiled=True),
        preferred_element_type=jnp.float32,
    )


def per_device(signal, conv_weight, conv_bias, ln_gain, ln_bias, w_space, w_time, w_out):
    kernel, bias_full, gain_full, shift_full = (
        lax.all_gather(conv_weight, "fsdp", axis=1, tiled=True),
        lax.all_gather(conv_bias, "fsdp", axis=0, tiled=True),
        lax.all_gather(ln_gain, "fsdp", axis=0, tiled=True),
        lax.all_gather(ln_bias, "fsdp", axis=0, tiled=True),
    )
    nights, channels, patch_count, samples = signal.shape
    model_width = kernel.shape[1]
    half_width = model_width // 2
    head_count = HEADS // 2
    head_size = half_width // head_count
    flat = signal.reshape(-1, samples)
    embed = (
        jnp.dot(flat, kernel, preferred_element_type=jnp.float32) + bias_full.astype(jnp.float32)
    ).astype(jnp.bfloat16)
    embed = lax.optimization_barrier(embed)
    normed = layer_norm(embed.astype(jnp.float32), gain_full, shift_full).astype(jnp.bfloat16)
    space_qkv = project(normed[:, :half_width], w_space).astype(jnp.bfloat16)
    space_qkv = space_qkv.reshape(channels, patch_count, 3, head_count, head_size).transpose(
        1, 0, 2, 3, 4
    )
    space_out = attend(space_qkv[:, :, 0], space_qkv[:, :, 1], space_qkv[:, :, 2])
    space_out = space_out.transpose(1, 0, 2, 3).reshape(-1, half_width)
    time_qkv = project(normed[:, half_width:], w_time).astype(jnp.bfloat16)
    time_qkv = time_qkv.reshape(channels, patch_count, 3, head_count, head_size)
    local_out = attend(
        lax.all_to_all(time_qkv[:, :, 0], "seq", split_axis=0, concat_axis=1, tiled=True),
        lax.all_to_all(time_qkv[:, :, 1], "seq", split_axis=0, concat_axis=1, tiled=True),
        lax.all_to_all(time_qkv[:, :, 2], "seq", split_axis=0, concat_axis=1, tiled=True),
    )
    time_out = lax.all_to_all(local_out, "seq", split_axis=1, concat_axis=0, tiled=True)
    joined = jnp.concatenate([space_out, time_out.reshape(-1, half_width)], axis=1)
    mixed = embed.astype(jnp.float32) + project(joined, w_out)
    return mixed.astype(jnp.bfloat16).reshape(nights, channels, patch_count, model_width)


RING = 8
CONV, PROJ, OUT = 0, 1, 2


def shard_at(position, core):
    position = lax.rem(position + 2 * RING, RING)
    y = position // 4
    z = jnp.where(y == 0, position, 7 - position)
    return (z * 2 + y) * 2 + core


def gather_kernel(
    sig_ref, conv_ref, proj_ref, out_ref,
    sig_full, conv_full, proj_full, out_full,
    ring_send, ring_recv, sib_send, sib_recv, x_send, x_recv, sibx_send, sibx_recv, own_sem, sig_sem,
):
    s = lax.axis_index("seq")
    f = lax.axis_index("fsdp")
    core = lax.rem(f, 2)
    chip = f // 2
    y = lax.rem(chip, 2)
    z = chip // 2
    r = jnp.where(y == 0, z, 7 - z)
    d = 1 - 2 * core
    ahead = {"seq": s, "fsdp": shard_at(r + d, core)}
    behind = {"seq": s, "fsdp": shard_at(r - d, core)}
    sibling = {"seq": s, "fsdp": f + d}
    across = {"seq": 1 - s, "fsdp": f}
    half = out_ref.shape[0] // 2
    width = conv_ref.shape[1]

    def place(kind, shard, side=None):
        if kind == CONV:
            return conv_full.at[:, pl.ds(pl.multiple_of(shard * width, width), width)]
        if kind == PROJ:
            return proj_full.at[shard]
        return out_full.at[shard, pl.ds(pl.multiple_of(side * half, half), half)]

    def own(kind):
        if kind == CONV:
            return conv_ref
        if kind == PROJ:
            return proj_ref
        return out_ref.at[pl.ds(pl.multiple_of(s * half, half), half)]

    def shard_of(k, c, direction):
        if k <= 4:
            return shard_at(r - k * direction, c)
        return shard_at(r + (k - 4) * direction, c)

    barrier = pltpu.get_barrier_semaphore()
    for other in (ahead, behind, sibling, across):
        pl.semaphore_signal(barrier, inc=1, device_id=other, device_id_type=MESH)
    pl.semaphore_wait(barrier, 4)

    sent = []

    def send(src, dst, send_sem, recv_sem, device):
        copy = pltpu.make_async_remote_copy(
            src_ref=src, dst_ref=dst, send_sem=send_sem, recv_sem=recv_sem,
            device_id=device, device_id_type=MESH,
        )
        copy.start()
        sent.append(copy)

    def arrive(dst, recv_sem):
        pltpu.make_async_remote_copy(
            src_ref=dst, dst_ref=dst, send_sem=recv_sem, recv_sem=recv_sem,
            device_id=sibling, device_id_type=MESH,
        ).wait_recv()

    def onward(kind, k, src):
        dst = place(kind, shard_of(k, core, d), s)
        if k < 4:
            send(src, dst, ring_send.at[kind, k + 1], ring_recv.at[kind, k + 1], ahead)
        if k == 0 or 5 <= k < 7:
            nxt = 5 if k == 0 else k + 1
            send(src, dst, ring_send.at[kind, nxt], ring_recv.at[kind, nxt], behind)
        if kind == OUT:
            send(src, dst, x_send.at[k], x_recv.at[k], across)
        send(src, dst, sib_send.at[kind, k], sib_recv.at[kind, k], sibling)

    def take(kind, k):
        dst = place(kind, shard_of(k, core, d), s)
        arrive(dst, ring_recv.at[kind, k])
        onward(kind, k, dst)

    def take_x(k):
        dst = place(OUT, shard_of(k, core, d), 1 - s)
        arrive(dst, x_recv.at[k])
        send(dst, dst, sibx_send.at[k], sibx_recv.at[k], sibling)

    send(sig_ref, sig_full.at[s], sig_sem.at[0], sig_sem.at[1], across)
    locals_ = [pltpu.make_async_copy(sig_ref, sig_full.at[s], own_sem.at[3])]
    locals_[0].start()
    for kind in (CONV, PROJ, OUT):
        onward(kind, 0, own(kind))
        mine = pltpu.make_async_copy(own(kind), place(kind, f, s), own_sem.at[kind])
        mine.start()
        locals_.append(mine)

    both = ((1, 5), (2, 6), (3, 7), (4,))
    order = (
        (CONV, 0), (CONV, 1), (PROJ, 0), (CONV, 2), (CONV, 3), (PROJ, 1), (OUT, 0),
        (PROJ, 2), (OUT, 1), (PROJ, 3), (OUT, 2), (OUT, 3),
    )
    for kind, step in order:
        for k in both[step]:
            take(kind, k)
        if kind == OUT:
            for k in both[step - 1] if step else (0,):
                take_x(k)
    take_x(4)
    for kind in (CONV, PROJ, OUT):
        for k in range(RING):
            arrive(place(kind, shard_of(k, 1 - core, -d), s), sib_recv.at[kind, k])
    for k in range(RING):
        arrive(place(OUT, shard_of(k, 1 - core, -d), 1 - s), sibx_recv.at[k])
    arrive(sig_full.at[1 - s], sig_sem.at[1])
    for copy in locals_:
        copy.wait()
    for copy in sent:
        copy.wait_send()


def gather_all(signal, conv, proj, out):
    dma = pltpu.SemaphoreType.DMA
    shards = 2 * RING
    return pl.pallas_call(
        gather_kernel,
        out_shape=(
            jax.ShapeDtypeStruct((2, *signal.shape), signal.dtype),
            jax.ShapeDtypeStruct((conv.shape[0], shards * conv.shape[1]), conv.dtype),
            jax.ShapeDtypeStruct((shards, *proj.shape), proj.dtype),
            jax.ShapeDtypeStruct((shards, *out.shape), out.dtype),
        ),
        in_specs=[pl.BlockSpec(memory_space=pl.ANY)] * 4,
        out_specs=[pl.BlockSpec(memory_space=pl.ANY)] * 4,
        scratch_shapes=[
            dma((3, 8)), dma((3, 8)), dma((3, 8)), dma((3, 8)),
            dma((8,)), dma((8,)), dma((8,)), dma((8,)), dma((4,)), dma((2,)),
        ],
        compiler_params=pltpu.CompilerParams(collective_id=0, has_side_effects=True),
    )(signal, conv, proj, out)


def split_by_branch(signal, conv_weight, conv_bias, ln_gain, ln_bias, w_space, w_time, w_out):
    s = lax.axis_index("seq")
    _, channels, patches, samples = signal.shape
    width = w_out.shape[1]
    half = width // 2
    heads = HEADS // 2
    head_size = half // heads
    tokens = channels * patches
    rows = jnp.stack([conv_bias, ln_gain, ln_bias])
    conv = jnp.concatenate([conv_weight, jnp.pad(rows, ((0, 13), (0, 0)))], axis=0)
    proj = jnp.where(s == 0, w_space, w_time)
    sig, conv, proj, out_w = gather_all(signal.reshape(tokens, samples), conv, proj, w_out)
    bias, gain, shift = (conv[samples + i].astype(jnp.float32) for i in range(3))
    embed = (
        jnp.dot(sig.reshape(-1, samples), conv[:samples], preferred_element_type=jnp.float32) + bias
    ).astype(jnp.bfloat16)
    embed = lax.optimization_barrier(embed)
    normed = layer_norm(embed.astype(jnp.float32), gain, shift).astype(jnp.bfloat16)
    normed = jnp.where(s == 0, normed[:, :half], normed[:, half:])
    qkv = jnp.dot(normed, proj.reshape(half, -1), preferred_element_type=jnp.float32)
    qkv = qkv.astype(jnp.bfloat16).reshape(2, channels, patches, 3, heads, head_size)

    def space(v):
        v = v.transpose(0, 2, 1, 3, 4, 5).reshape(2 * patches, channels, 3, heads, head_size)
        v = attend(v[:, :, 0], v[:, :, 1], v[:, :, 2]).reshape(2, patches, channels, half)
        return v.transpose(0, 2, 1, 3).reshape(2, tokens, half)

    def time(v):
        v = v.transpose(1, 0, 2, 3, 4, 5).reshape(channels, 2 * patches, 3, heads, head_size)
        v = attend(v[:, :, 0], v[:, :, 1], v[:, :, 2]).reshape(channels, 2, patches, half)
        return v.transpose(1, 0, 2, 3).reshape(2, tokens, half)

    result = lax.cond(s == 0, space, time, qkv)
    theirs = lax.ppermute(result[1 - s], "seq", [(0, 1), (1, 0)])
    mine = result[s]
    joined = jnp.concatenate(
        [jnp.where(s == 0, mine, theirs), jnp.where(s == 0, theirs, mine)], axis=1
    )
    residual = embed.reshape(2, tokens, width)[s].astype(jnp.float32)
    mixed = residual + jnp.dot(joined, out_w.reshape(width, width), preferred_element_type=jnp.float32)
    return mixed.astype(jnp.bfloat16).reshape(1, channels, patches, width)


def solution(mesh):
    in_specs = (
        P("fsdp", None, "seq", None),
        P(None, "fsdp"),
        P("fsdp"),
        P("fsdp"),
        P("fsdp"),
        P("fsdp", None),
        P("fsdp", None),
        P("fsdp", None),
    )
    out_specs = P("fsdp", None, "seq", None)
    whole_night = mesh.shape["seq"] == 2 and mesh.shape["fsdp"] == 2 * RING
    body = split_by_branch if whole_night else per_device
    return jax.shard_map(
        body, mesh=mesh, in_specs=in_specs, out_specs=out_specs, check_vma=False
    )
```

```python
import math

import jax
import jax.numpy as jnp
import ml_dtypes
import numpy as np
from jax import lax
from jax.experimental import pallas as pl
from jax.experimental.pallas import tpu as pltpu
from jax.sharding import PartitionSpec as P

HEADS = 16
MESH = pl.DeviceIdType.MESH


def layer_norm(values, gain, shift):
    mean = jnp.mean(values, axis=-1, keepdims=True)
    centred = values - mean
    variance = jnp.mean(centred * centred, axis=-1, keepdims=True)
    return centred * lax.rsqrt(variance + 1e-05) * gain.astype(jnp.float32) + shift.astype(
        jnp.float32
    )


def attend(queries, keys_in, values_in):
    scale = 1.0 / math.sqrt(queries.shape[-1])
    scores = (
        jnp.einsum("bqhd,bkhd->bhqk", queries, keys_in, preferred_element_type=jnp.float32) * scale
    )
    highest = jnp.max(scores, axis=-1, keepdims=True)
    expo = jnp.exp(scores - highest)
    probs = (expo / jnp.sum(expo, axis=-1, keepdims=True)).astype(jnp.bfloat16)
    result = jnp.einsum("bhqk,bkhd->bqhd", probs, values_in, preferred_element_type=jnp.float32)
    return result.astype(jnp.bfloat16)


def project(features, weight):
    return jnp.dot(
        features,
        lax.all_gather(weight, "fsdp", axis=0, tiled=True),
        preferred_element_type=jnp.float32,
    )


def per_device(signal, conv_weight, conv_bias, ln_gain, ln_bias, w_space, w_time, w_out):
    kernel, bias_full, gain_full, shift_full = (
        lax.all_gather(conv_weight, "fsdp", axis=1, tiled=True),
        lax.all_gather(conv_bias, "fsdp", axis=0, tiled=True),
        lax.all_gather(ln_gain, "fsdp", axis=0, tiled=True),
        lax.all_gather(ln_bias, "fsdp", axis=0, tiled=True),
    )
    nights, channels, patch_count, samples = signal.shape
    model_width = kernel.shape[1]
    half_width = model_width // 2
    head_count = HEADS // 2
    head_size = half_width // head_count
    flat = signal.reshape(-1, samples)
    embed = (
        jnp.dot(flat, kernel, preferred_element_type=jnp.float32) + bias_full.astype(jnp.float32)
    ).astype(jnp.bfloat16)
    embed = lax.optimization_barrier(embed)
    normed = layer_norm(embed.astype(jnp.float32), gain_full, shift_full).astype(jnp.bfloat16)
    space_qkv = project(normed[:, :half_width], w_space).astype(jnp.bfloat16)
    space_qkv = space_qkv.reshape(channels, patch_count, 3, head_count, head_size).transpose(
        1, 0, 2, 3, 4
    )
    space_out = attend(space_qkv[:, :, 0], space_qkv[:, :, 1], space_qkv[:, :, 2])
    space_out = space_out.transpose(1, 0, 2, 3).reshape(-1, half_width)
    time_qkv = project(normed[:, half_width:], w_time).astype(jnp.bfloat16)
    time_qkv = time_qkv.reshape(channels, patch_count, 3, head_count, head_size)
    local_out = attend(
        lax.all_to_all(time_qkv[:, :, 0], "seq", split_axis=0, concat_axis=1, tiled=True),
        lax.all_to_all(time_qkv[:, :, 1], "seq", split_axis=0, concat_axis=1, tiled=True),
        lax.all_to_all(time_qkv[:, :, 2], "seq", split_axis=0, concat_axis=1, tiled=True),
    )
    time_out = lax.all_to_all(local_out, "seq", split_axis=1, concat_axis=0, tiled=True)
    joined = jnp.concatenate([space_out, time_out.reshape(-1, half_width)], axis=1)
    mixed = embed.astype(jnp.float32) + project(joined, w_out)
    return mixed.astype(jnp.bfloat16).reshape(nights, channels, patch_count, model_width)


RING = 8
CONV, PROJ, OUT = 0, 1, 2


def shard_at(position, core):
    position = lax.rem(position + 2 * RING, RING)
    y = position // 4
    z = jnp.where(y == 0, position, 7 - position)
    return (z * 2 + y) * 2 + core


ROWS = 160


def night_kernel(
    sig_ref, conv_ref, space_ref, time_ref, out_ref, to_role_ref, to_own_ref, mask_a_ref, mask_b_ref,
    mixed_ref,
    sig_full, sig_role, conv_full, proj_full, out_full, normed, qkv, result, outgoing, joined, total,
    ring_send, ring_recv, sib_send, sib_recv, x_send, x_recv, sibx_send, sibx_recv, own_sem, sig_sem,
    swap_send, swap_recv,
):
    s = lax.axis_index("seq")
    f = lax.axis_index("fsdp")
    core = lax.rem(f, 2)
    chip = f // 2
    y = lax.rem(chip, 2)
    z = chip // 2
    r = jnp.where(y == 0, z, 7 - z)
    d = 1 - 2 * core
    ahead = {"seq": s, "fsdp": shard_at(r + d, core)}
    behind = {"seq": s, "fsdp": shard_at(r - d, core)}
    sibling = {"seq": s, "fsdp": f + d}
    across = {"seq": 1 - s, "fsdp": f}
    depth, width = out_ref.shape
    half = width // 2
    cols = conv_ref.shape[1]
    proj_depth = space_ref.shape[0]
    tokens, samples = sig_ref.shape
    quarter = depth // 4
    head_size = width // HEADS
    pair = 2 * head_size

    def place(kind, shard):
        if kind == CONV:
            return conv_full.at[:, pl.ds(pl.multiple_of(shard * cols, cols), cols)]
        if kind == PROJ:
            return proj_full.at[pl.ds(pl.multiple_of(shard * proj_depth, proj_depth), proj_depth)]
        start = pl.multiple_of(shard * depth + s * quarter, quarter)
        return out_full.at[pl.ds(start, 3 * quarter)]

    def place_x(shard, side):
        start = pl.multiple_of(shard * depth + side * 3 * quarter, quarter)
        return out_full.at[pl.ds(start, quarter)]

    def shard_of(k, c, direction):
        if k <= 4:
            return shard_at(r - k * direction, c)
        return shard_at(r + (k - 4) * direction, c)

    own_conv = pltpu.make_async_copy(conv_ref, place(CONV, f), own_sem.at[0])
    own_proj_a = pltpu.make_async_copy(space_ref, place(PROJ, f), own_sem.at[1])
    own_proj_b = pltpu.make_async_copy(time_ref, place(PROJ, f), own_sem.at[1])
    own_rows = pl.ds(pl.multiple_of(f * depth, depth), depth)
    own_out = pltpu.make_async_copy(out_ref, out_full.at[own_rows], own_sem.at[2])
    own_conv.start()
    pl.when(s == 0)(own_proj_a.start)
    pl.when(s == 1)(own_proj_b.start)
    own_out.start()

    barrier = pltpu.get_barrier_semaphore()
    for other in (ahead, behind, sibling, across):
        pl.semaphore_signal(barrier, inc=1, device_id=other, device_id_type=MESH)
    pl.semaphore_wait(barrier, 4)

    sent = []

    def send(src, dst, send_sem, recv_sem, device):
        copy = pltpu.make_async_remote_copy(
            src_ref=src, dst_ref=dst, send_sem=send_sem, recv_sem=recv_sem,
            device_id=device, device_id_type=MESH,
        )
        copy.start()
        sent.append(copy)

    def arrive(dst, recv_sem):
        pltpu.make_async_remote_copy(
            src_ref=dst, dst_ref=dst, send_sem=recv_sem, recv_sem=recv_sem,
            device_id=sibling, device_id_type=MESH,
        ).wait_recv()

    def onward(kind, k):
        shard = shard_of(k, core, d)
        dst = place(kind, shard)
        if k < 4:
            send(dst, dst, ring_send.at[kind, k + 1], ring_recv.at[kind, k + 1], ahead)
        if k == 0 or 5 <= k < 7:
            nxt = 5 if k == 0 else k + 1
            send(dst, dst, ring_send.at[kind, nxt], ring_recv.at[kind, nxt], behind)
        if kind == OUT and k == 0:
            quart = place_x(shard, 1 - s)
            send(quart, quart, sibx_send.at[0], sibx_recv.at[0], sibling)
        elif kind == OUT:
            quart = place_x(shard, s)
            send(quart, quart, x_send.at[k], x_recv.at[k], across)
        send(dst, dst, sib_send.at[kind, k], sib_recv.at[kind, k], sibling)

    both = ((1, 5), (2, 6), (3, 7), (4,))

    def step(kind, at):
        for k in both[at]:
            arrive(place(kind, shard_of(k, core, d)), ring_recv.at[kind, k])
            onward(kind, k)

    def step_x(*slots):
        for k in slots:
            dst = place_x(shard_of(k, core, d), 1 - s)
            arrive(dst, x_recv.at[k])
            send(dst, dst, sibx_send.at[k], sibx_recv.at[k], sibling)

    def from_sibling(kind, k):
        arrive(place(kind, shard_of(k, 1 - core, -d)), sib_recv.at[kind, k])

    def embed(x):
        e = jnp.dot(x, conv_full[:samples], preferred_element_type=jnp.float32)
        return (e + conv_full[samples : samples + 1].astype(jnp.float32)).astype(jnp.bfloat16)

    def norm_rows(first, count):
        @pl.loop(first, first + count)
        def _(i):
            rows = pl.ds(pl.multiple_of(i * ROWS, ROWS), ROWS)
            e = embed(sig_role[rows]).astype(jnp.float32)
            mean = jnp.mean(e, axis=-1, keepdims=True)
            centred = e - mean
            variance = jnp.mean(centred * centred, axis=-1, keepdims=True)
            inverse = lax.rsqrt(variance + 1e-05)

            def keep(lo):
                part = slice(lo, lo + half)
                gain = conv_full[samples + 1 : samples + 2, part].astype(jnp.float32)
                shift = conv_full[samples + 2 : samples + 3, part].astype(jnp.float32)
                normed[rows] = (centred[:, part] * inverse * gain + shift).astype(jnp.bfloat16)

            pl.when(s == 0)(lambda: keep(0))
            pl.when(s == 1)(lambda: keep(half))

    def start_total():
        @pl.loop(0, tokens // ROWS)
        def _(i):
            rows = pl.ds(pl.multiple_of(i * ROWS, ROWS), ROWS)
            total[rows] = embed(sig_ref[rows]).astype(jnp.float32)

    def attend_rows(q, k, v, allowed):
        scores = lax.dot_general(
            q, k, (((1,), (1,)), ((), ())), preferred_element_type=jnp.float32
        ) * (1.0 / math.sqrt(head_size))
        scores = jnp.where(allowed, scores, -jnp.inf)
        highest = jnp.max(scores, axis=-1, keepdims=True)
        expo = jnp.exp(scores - highest)
        probs = (expo / jnp.sum(expo, axis=-1, keepdims=True)).astype(jnp.bfloat16)
        return jnp.dot(probs, v, preferred_element_type=jnp.float32).astype(jnp.bfloat16)

    def heads(j):
        @pl.loop(0, 2 * tokens // (2 * ROWS))
        def _(i):
            rows = pl.ds(pl.multiple_of(i * 2 * ROWS, 2 * ROWS), 2 * ROWS)
            for part in range(3):
                w = proj_full[:, part * half + j * pair : part * half + (j + 1) * pair]
                value = jnp.dot(normed[rows], w, preferred_element_type=jnp.float32)
                qkv[rows, part * pair : (part + 1) * pair] = value.astype(jnp.bfloat16)

        at = slice(j * pair, (j + 1) * pair)

        @pl.when(s == 0)
        def _():
            count = mask_a_ref.shape[0]

            @pl.loop(0, 2 * tokens // count)
            def _(g):
                rows = pl.ds(pl.multiple_of(g * count, count), count)
                allowed = mask_a_ref[...] > 0
                for h in range(2):
                    q, k, v = (
                        qkv[rows, part * pair + h * head_size : part * pair + (h + 1) * head_size]
                        for part in range(3)
                    )
                    to = j * pair + h * head_size
                    result[rows, to : to + head_size] = attend_rows(q, k, v, allowed)

        @pl.when(s == 1)
        def _():
            count = mask_b_ref.shape[0] // 2

            @pl.loop(0, tokens // count)
            def _(g):
                first = pl.ds(pl.multiple_of(g * count, 16), count)
                second = pl.ds(pl.multiple_of(tokens + g * count, 16), count)
                allowed = mask_b_ref[...] > 0
                for h in range(2):
                    q, k, v = (
                        jnp.concatenate(
                            [
                                qkv[rows, part * pair + h * head_size : part * pair + (h + 1) * head_size]
                                for rows in (first, second)
                            ],
                            axis=0,
                        )
                        for part in range(3)
                    )
                    to = j * pair + h * head_size
                    value = attend_rows(q, k, v, allowed)
                    result[first, to : to + head_size] = value[:count]
                    result[second, to : to + head_size] = value[count:]

        mine = pl.ds(pl.multiple_of(s * half + j * pair, pair), pair)

        def reorder(side):
            rows = pl.ds(pl.multiple_of(side * tokens, tokens), tokens)
            return jnp.dot(
                to_own_ref[...], result[rows, at], preferred_element_type=jnp.float32
            ).astype(jnp.bfloat16)

        outgoing[:, at] = reorder(1 - s)
        send(outgoing.at[:, at], joined.at[:, mine], swap_send.at[j], swap_recv.at[j], across)
        joined[:, mine] = reorder(s)

    def add_chip(k, last=False):
        at = pl.ds(pl.multiple_of((shard_of(k, core, d) // 2) * 2 * depth, 2 * depth), 2 * depth)

        @pl.loop(0, tokens // ROWS)
        def _(i):
            rows = pl.ds(pl.multiple_of(i * ROWS, ROWS), ROWS)
            value = total[rows] + jnp.dot(
                joined[rows, at], out_full[at, :], preferred_element_type=jnp.float32
            )
            if last:
                mixed_ref[rows] = value.astype(jnp.bfloat16)
            else:
                total[rows] = value

    send(sig_ref, sig_full.at[s], sig_sem.at[0], sig_sem.at[1], across)
    own_conv.wait()
    onward(CONV, 0)
    pl.when(s == 0)(own_proj_a.wait)
    pl.when(s == 1)(own_proj_b.wait)
    onward(PROJ, 0)
    own_out.wait()
    step(CONV, 0)
    step(CONV, 1)
    sig_full[s] = sig_ref[...]
    step(CONV, 2)
    step(CONV, 3)
    step(PROJ, 0)
    onward(OUT, 0)
    arrive(sig_full.at[1 - s], sig_sem.at[1])
    for side in range(2):
        sig_role[side * tokens : (side + 1) * tokens] = jnp.dot(
            to_role_ref[...], sig_full[side], preferred_element_type=jnp.float32
        ).astype(jnp.bfloat16)
    for k in range(RING):
        from_sibling(CONV, k)
    norm_rows(0, 3)
    step(PROJ, 1)
    norm_rows(3, 3)
    step(PROJ, 2)
    step(OUT, 0)
    norm_rows(6, 2)
    start_total()
    step(PROJ, 3)
    step(OUT, 1)
    step_x(1, 5)
    for k in range(RING):
        from_sibling(PROJ, k)
    heads(0)
    step(OUT, 2)
    step_x(2, 6)
    heads(1)
    step(OUT, 3)
    step_x(3, 7)
    heads(2)
    step_x(4)
    heads(3)
    for j in range(HEADS // 4):
        theirs = pl.ds(pl.multiple_of((1 - s) * half + j * pair, pair), pair)
        arrive(joined.at[:, theirs], swap_recv.at[j])
    slots = (0, 1, 5, 2, 6, 3, 7, 4)
    partner = {0: 0, 1: 5, 5: 1, 2: 6, 6: 2, 3: 7, 7: 3, 4: 4}
    for k in slots:
        from_sibling(OUT, partner[k])
        arrive(place_x(shard_of(partner[k], 1 - core, -d), 1 - s), sibx_recv.at[partner[k]])
        add_chip(k, last=k == 4)
    for copy in sent:
        copy.wait_send()


def split_by_branch(signal, conv_weight, conv_bias, ln_gain, ln_bias, w_space, w_time, w_out):
    s = lax.axis_index("seq")
    _, channels, patches, samples = signal.shape
    width = w_out.shape[1]
    half = width // 2
    tokens = channels * patches
    shards = 2 * RING
    rows = jnp.stack([conv_bias, ln_gain, ln_bias])
    conv = jnp.concatenate([conv_weight, jnp.pad(rows, ((0, 13), (0, 0)))], axis=0)
    order = np.arange(tokens).reshape(channels, patches)
    natural = np.eye(tokens, dtype=ml_dtypes.bfloat16)
    patch_major = natural[order.T.reshape(-1)]
    to_role = jnp.where(s == 0, jnp.asarray(patch_major), jnp.asarray(natural))
    to_own = jnp.where(s == 0, jnp.asarray(patch_major.T), jnp.asarray(natural))
    patch_of = np.arange(2 * channels) // channels
    mask_a = (patch_of[:, None] == patch_of[None]).astype(np.float32)
    channel_of = np.tile(np.arange(8 * patches) // patches, 2)
    mask_b = (channel_of[:, None] == channel_of[None]).astype(np.float32)
    dma = pltpu.SemaphoreType.DMA
    vmem = pl.BlockSpec(memory_space=pltpu.VMEM)
    anywhere = pl.BlockSpec(memory_space=pl.ANY)
    bf16 = jnp.bfloat16
    flops = 4 * tokens * (width * samples + half * 3 * half + width * width // 2)
    mixed = pl.pallas_call(
        night_kernel,
        out_shape=jax.ShapeDtypeStruct((tokens, width), bf16),
        in_specs=[vmem, anywhere, anywhere, anywhere, anywhere, vmem, vmem, vmem, vmem],
        out_specs=vmem,
        scratch_shapes=[
            pltpu.VMEM((2, tokens, samples), bf16),
            pltpu.VMEM((2 * tokens, samples), bf16),
            pltpu.VMEM((conv.shape[0], width), bf16),
            pltpu.VMEM((shards * w_space.shape[0], w_space.shape[1]), bf16),
            pltpu.VMEM((shards * w_out.shape[0], width), bf16),
            pltpu.VMEM((2 * tokens, half), bf16),
            pltpu.VMEM((2 * tokens, 6 * width // HEADS), bf16),
            pltpu.VMEM((2 * tokens, half), bf16),
            pltpu.VMEM((tokens, half), bf16),
            pltpu.VMEM((tokens, width), bf16),
            pltpu.VMEM((tokens, width), jnp.float32),
            dma((3, 8)), dma((3, 8)), dma((3, 8)), dma((3, 8)),
            dma((8,)), dma((8,)), dma((8,)), dma((8,)), dma((3,)), dma((2,)), dma((4,)), dma((4,)),
        ],
        compiler_params=pltpu.CompilerParams(
            collective_id=0, has_side_effects=True, vmem_limit_bytes=60 * 2**20
        ),
        cost_estimate=pl.CostEstimate(flops=flops, bytes_accessed=2**23, transcendentals=2**21),
    )(signal.reshape(tokens, samples), conv, w_space, w_time, w_out, to_role, to_own,
      jnp.asarray(mask_a), jnp.asarray(mask_b))
    return mixed.reshape(1, channels, patches, width)


def solution(mesh):
    in_specs = (
        P("fsdp", None, "seq", None),
        P(None, "fsdp"),
        P("fsdp"),
        P("fsdp"),
        P("fsdp"),
        P("fsdp", None),
        P("fsdp", None),
        P("fsdp", None),
    )
    out_specs = P("fsdp", None, "seq", None)
    whole_night = mesh.shape["seq"] == 2 and mesh.shape["fsdp"] == 2 * RING
    body = split_by_branch if whole_night else per_device
    return jax.shard_map(
        body, mesh=mesh, in_specs=in_specs, out_specs=out_specs, check_vma=False
    )
```

```python
import functools
import math

import jax
import jax.numpy as jnp
import numpy as np
from jax import lax
from jax.experimental import pallas as pl
from jax.experimental.pallas import tpu as pltpu
from jax.sharding import PartitionSpec as P

HEADS = 16
MESH = pl.DeviceIdType.MESH


def layer_norm(values, gain, shift):
    mean = jnp.mean(values, axis=-1, keepdims=True)
    centred = values - mean
    variance = jnp.mean(centred * centred, axis=-1, keepdims=True)
    return centred * lax.rsqrt(variance + 1e-05) * gain.astype(jnp.float32) + shift.astype(
        jnp.float32
    )


def attend(queries, keys_in, values_in):
    scale = 1.0 / math.sqrt(queries.shape[-1])
    scores = (
        jnp.einsum("bqhd,bkhd->bhqk", queries, keys_in, preferred_element_type=jnp.float32) * scale
    )
    highest = jnp.max(scores, axis=-1, keepdims=True)
    expo = jnp.exp(scores - highest)
    probs = (expo / jnp.sum(expo, axis=-1, keepdims=True)).astype(jnp.bfloat16)
    result = jnp.einsum("bhqk,bkhd->bqhd", probs, values_in, preferred_element_type=jnp.float32)
    return result.astype(jnp.bfloat16)


def project(features, weight):
    return jnp.dot(
        features,
        lax.all_gather(weight, "fsdp", axis=0, tiled=True),
        preferred_element_type=jnp.float32,
    )


def per_device(signal, conv_weight, conv_bias, ln_gain, ln_bias, w_space, w_time, w_out):
    kernel, bias_full, gain_full, shift_full = (
        lax.all_gather(conv_weight, "fsdp", axis=1, tiled=True),
        lax.all_gather(conv_bias, "fsdp", axis=0, tiled=True),
        lax.all_gather(ln_gain, "fsdp", axis=0, tiled=True),
        lax.all_gather(ln_bias, "fsdp", axis=0, tiled=True),
    )
    nights, channels, patch_count, samples = signal.shape
    model_width = kernel.shape[1]
    half_width = model_width // 2
    head_count = HEADS // 2
    head_size = half_width // head_count
    flat = signal.reshape(-1, samples)
    embed = (
        jnp.dot(flat, kernel, preferred_element_type=jnp.float32) + bias_full.astype(jnp.float32)
    ).astype(jnp.bfloat16)
    embed = lax.optimization_barrier(embed)
    normed = layer_norm(embed.astype(jnp.float32), gain_full, shift_full).astype(jnp.bfloat16)
    space_qkv = project(normed[:, :half_width], w_space).astype(jnp.bfloat16)
    space_qkv = space_qkv.reshape(channels, patch_count, 3, head_count, head_size).transpose(
        1, 0, 2, 3, 4
    )
    space_out = attend(space_qkv[:, :, 0], space_qkv[:, :, 1], space_qkv[:, :, 2])
    space_out = space_out.transpose(1, 0, 2, 3).reshape(-1, half_width)
    time_qkv = project(normed[:, half_width:], w_time).astype(jnp.bfloat16)
    time_qkv = time_qkv.reshape(channels, patch_count, 3, head_count, head_size)
    local_out = attend(
        lax.all_to_all(time_qkv[:, :, 0], "seq", split_axis=0, concat_axis=1, tiled=True),
        lax.all_to_all(time_qkv[:, :, 1], "seq", split_axis=0, concat_axis=1, tiled=True),
        lax.all_to_all(time_qkv[:, :, 2], "seq", split_axis=0, concat_axis=1, tiled=True),
    )
    time_out = lax.all_to_all(local_out, "seq", split_axis=1, concat_axis=0, tiled=True)
    joined = jnp.concatenate([space_out, time_out.reshape(-1, half_width)], axis=1)
    mixed = embed.astype(jnp.float32) + project(joined, w_out)
    return mixed.astype(jnp.bfloat16).reshape(nights, channels, patch_count, model_width)


RING = 8
CONV, PROJ_A, PROJ_B, OUT_A, OUT_B = range(5)


def shard_at(position, core):
    position = lax.rem(position + 2 * RING, RING)
    y = position // 4
    z = jnp.where(y == 0, position, 7 - position)
    return (z * 2 + y) * 2 + core


ROWS = 160


def night_kernel(
    channels, patches, sig_ref, conv_ref, space_ref, time_ref, out_ref, mask_a_ref, mask_b_ref,
    mixed_ref,
    sig_full, sig_role, conv_full, proj_full, out_full, normed, qkv, result, outgoing, joined, total,
    to_role_ref, to_own_ref,
    ring_send, ring_recv, sib_send, sib_recv, x_send, x_recv, sibx_send, sibx_recv, own_sem, sig_sem,
    swap_send, swap_recv,
):
    s = lax.axis_index("seq")
    f = lax.axis_index("fsdp")
    core = lax.rem(f, 2)
    chip = f // 2
    y = lax.rem(chip, 2)
    z = chip // 2
    r = jnp.where(y == 0, z, 7 - z)
    d = 1 - 2 * core
    ahead = {"seq": s, "fsdp": shard_at(r + d, core)}
    behind = {"seq": s, "fsdp": shard_at(r - d, core)}
    sibling = {"seq": s, "fsdp": f + d}
    across = {"seq": 1 - s, "fsdp": f}
    depth, width = out_ref.shape
    half = width // 2
    cols = conv_ref.shape[1]
    proj_depth = space_ref.shape[0]
    tokens, samples = sig_ref.shape
    quarter = depth // 4
    head_size = width // HEADS
    pair = 2 * head_size

    def place(kind, shard):
        if kind == CONV:
            return conv_full.at[:, pl.ds(pl.multiple_of(shard * cols, cols), cols)]
        if kind in (PROJ_A, PROJ_B):
            count = proj_depth // 2
            start = pl.multiple_of(shard * proj_depth + (kind - PROJ_A) * count, count)
            return proj_full.at[pl.ds(start, count)]
        count = 3 * depth // 8
        first = s * (depth - count) if kind == OUT_A else count - s * (2 * count - 5 * depth // 8)
        return out_full.at[pl.ds(pl.multiple_of(shard * depth + first, 16), count)]

    def place_x(shard, side):
        start = pl.multiple_of(shard * depth + side * 3 * quarter, quarter)
        return out_full.at[pl.ds(start, quarter)]

    def shard_of(k, c, direction):
        if k <= 4:
            return shard_at(r - k * direction, c)
        return shard_at(r + (k - 4) * direction, c)

    own_conv = pltpu.make_async_copy(conv_ref, place(CONV, f), own_sem.at[0])
    own_proj_rows = pl.ds(pl.multiple_of(f * proj_depth, proj_depth), proj_depth)
    own_proj_a = pltpu.make_async_copy(space_ref, proj_full.at[own_proj_rows], own_sem.at[1])
    own_proj_b = pltpu.make_async_copy(time_ref, proj_full.at[own_proj_rows], own_sem.at[1])
    own_rows = pl.ds(pl.multiple_of(f * depth, depth), depth)
    own_out = pltpu.make_async_copy(out_ref, out_full.at[own_rows], own_sem.at[2])
    own_conv.start()
    pl.when(s == 0)(own_proj_a.start)
    pl.when(s == 1)(own_proj_b.start)
    own_out.start()

    barrier = pltpu.get_barrier_semaphore()
    for other in (ahead, behind, sibling, across):
        pl.semaphore_signal(barrier, inc=1, device_id=other, device_id_type=MESH)
    pl.semaphore_wait(barrier, 4)

    sent = []

    def send(src, dst, send_sem, recv_sem, device):
        copy = pltpu.make_async_remote_copy(
            src_ref=src, dst_ref=dst, send_sem=send_sem, recv_sem=recv_sem,
            device_id=device, device_id_type=MESH,
        )
        copy.start()
        sent.append(copy)

    def arrive(dst, recv_sem):
        pltpu.make_async_remote_copy(
            src_ref=dst, dst_ref=dst, send_sem=recv_sem, recv_sem=recv_sem,
            device_id=sibling, device_id_type=MESH,
        ).wait_recv()

    def onward(kind, k):
        shard = shard_of(k, core, d)
        dst = place(kind, shard)
        if k < 4:
            send(dst, dst, ring_send.at[kind, k + 1], ring_recv.at[kind, k + 1], ahead)
        if k == 0 or 5 <= k < 7:
            nxt = 5 if k == 0 else k + 1
            send(dst, dst, ring_send.at[kind, nxt], ring_recv.at[kind, nxt], behind)
        if kind == OUT_A and k == 0:
            quart = place_x(shard, 1 - s)
            send(quart, quart, sibx_send.at[0], sibx_recv.at[0], sibling)
        elif kind == OUT_A:
            quart = place_x(shard, s)
            send(quart, quart, x_send.at[k], x_recv.at[k], across)
        send(dst, dst, sib_send.at[kind, k], sib_recv.at[kind, k], sibling)

    both = ((1, 5), (2, 6), (3, 7), (4,))

    def step(kind, at):
        for k in both[at]:
            arrive(place(kind, shard_of(k, core, d)), ring_recv.at[kind, k])
            onward(kind, k)

    def step_x(*slots):
        for k in slots:
            dst = place_x(shard_of(k, core, d), 1 - s)
            arrive(dst, x_recv.at[k])
            send(dst, dst, sibx_send.at[k], sibx_recv.at[k], sibling)

    def from_sibling(kind, k):
        arrive(place(kind, shard_of(k, 1 - core, -d)), sib_recv.at[kind, k])

    def set_orders():
        row = lax.broadcasted_iota(jnp.int32, (tokens, 1), 0)
        col = lax.broadcasted_iota(jnp.int32, (tokens, tokens), 1)
        source = lax.rem(row, patches) * channels + lax.div(row, patches)
        to_role_ref[...] = (jnp.where(s == 0, row, source) == col).astype(jnp.bfloat16)
        target = lax.rem(row, channels) * patches + lax.div(row, channels)
        to_own_ref[...] = (jnp.where(s == 0, row, target) == col).astype(jnp.bfloat16)

    def embed(x):
        e = jnp.dot(x, conv_full[:samples], preferred_element_type=jnp.float32)
        return (e + conv_full[samples : samples + 1].astype(jnp.float32)).astype(jnp.bfloat16)

    def norm_rows(first, count):
        @pl.loop(first, first + count)
        def _(i):
            rows = pl.ds(pl.multiple_of(i * ROWS, ROWS), ROWS)
            e = embed(sig_role[rows]).astype(jnp.float32)
            mean = jnp.mean(e, axis=-1, keepdims=True)
            centred = e - mean
            variance = jnp.mean(centred * centred, axis=-1, keepdims=True)
            inverse = lax.rsqrt(variance + 1e-05)

            def keep(lo):
                part = slice(lo, lo + half)
                gain = conv_full[samples + 1 : samples + 2, part].astype(jnp.float32)
                shift = conv_full[samples + 2 : samples + 3, part].astype(jnp.float32)
                normed[rows] = (centred[:, part] * inverse * gain + shift).astype(jnp.bfloat16)

            pl.when(s == 0)(lambda: keep(0))
            pl.when(s == 1)(lambda: keep(half))

    def start_total():
        @pl.loop(0, tokens // ROWS)
        def _(i):
            rows = pl.ds(pl.multiple_of(i * ROWS, ROWS), ROWS)
            total[rows] = embed(sig_ref[rows]).astype(jnp.float32)

    def attend_rows(q, k, v, allowed):
        scores = lax.dot_general(
            q, k, (((1,), (1,)), ((), ())), preferred_element_type=jnp.float32
        ) * (1.0 / math.sqrt(head_size))
        scores = jnp.where(allowed, scores, -jnp.inf)
        highest = jnp.max(scores, axis=-1, keepdims=True)
        expo = jnp.exp(scores - highest)
        probs = (expo / jnp.sum(expo, axis=-1, keepdims=True)).astype(jnp.bfloat16)
        return jnp.dot(probs, v, preferred_element_type=jnp.float32).astype(jnp.bfloat16)

    def heads(j, between=lambda: None):
        @pl.loop(0, 2 * tokens // (2 * ROWS))
        def _(i):
            rows = pl.ds(pl.multiple_of(i * 2 * ROWS, 2 * ROWS), 2 * ROWS)
            for part in range(3):
                w = proj_full[:, part * half + j * pair : part * half + (j + 1) * pair]
                value = jnp.dot(normed[rows], w, preferred_element_type=jnp.float32)
                qkv[rows, part * pair : (part + 1) * pair] = value.astype(jnp.bfloat16)

        between()
        at = slice(j * pair, (j + 1) * pair)

        @pl.when(s == 0)
        def _():
            count = mask_a_ref.shape[0]

            @pl.loop(0, 2 * tokens // count)
            def _(g):
                rows = pl.ds(pl.multiple_of(g * count, count), count)
                allowed = mask_a_ref[...] > 0
                for h in range(2):
                    q, k, v = (
                        qkv[rows, part * pair + h * head_size : part * pair + (h + 1) * head_size]
                        for part in range(3)
                    )
                    to = j * pair + h * head_size
                    result[rows, to : to + head_size] = attend_rows(q, k, v, allowed)

        @pl.when(s == 1)
        def _():
            count = mask_b_ref.shape[0] // 2

            @pl.loop(0, tokens // count)
            def _(g):
                first = pl.ds(pl.multiple_of(g * count, 16), count)
                second = pl.ds(pl.multiple_of(tokens + g * count, 16), count)
                allowed = mask_b_ref[...] > 0
                for h in range(2):
                    q, k, v = (
                        jnp.concatenate(
                            [
                                qkv[rows, part * pair + h * head_size : part * pair + (h + 1) * head_size]
                                for rows in (first, second)
                            ],
                            axis=0,
                        )
                        for part in range(3)
                    )
                    to = j * pair + h * head_size
                    value = attend_rows(q, k, v, allowed)
                    result[first, to : to + head_size] = value[:count]
                    result[second, to : to + head_size] = value[count:]

        mine = pl.ds(pl.multiple_of(s * half + j * pair, pair), pair)

        def reorder(side):
            rows = pl.ds(pl.multiple_of(side * tokens, tokens), tokens)
            return jnp.dot(
                to_own_ref[...], result[rows, at], preferred_element_type=jnp.float32
            ).astype(jnp.bfloat16)

        outgoing[:, at] = reorder(1 - s)
        send(outgoing.at[:, at], joined.at[:, mine], swap_send.at[j], swap_recv.at[j], across)
        joined[:, mine] = reorder(s)

    def add_chip(k, last=False):
        at = pl.ds(pl.multiple_of((shard_of(k, core, d) // 2) * 2 * depth, 2 * depth), 2 * depth)

        @pl.loop(0, tokens // ROWS)
        def _(i):
            rows = pl.ds(pl.multiple_of(i * ROWS, ROWS), ROWS)
            value = total[rows] + jnp.dot(
                joined[rows, at], out_full[at, :], preferred_element_type=jnp.float32
            )
            if last:
                mixed_ref[rows] = value.astype(jnp.bfloat16)
            else:
                total[rows] = value

    send(sig_ref, sig_full.at[s], sig_sem.at[0], sig_sem.at[1], across)
    own_conv.wait()
    onward(CONV, 0)
    pl.when(s == 0)(own_proj_a.wait)
    pl.when(s == 1)(own_proj_b.wait)
    onward(PROJ_A, 0)
    onward(PROJ_B, 0)
    own_out.wait()
    set_orders()
    step(CONV, 0)
    step(CONV, 1)
    sig_full[s] = sig_ref[...]
    step(PROJ_A, 0)
    step(CONV, 2)
    step(PROJ_B, 0)
    step(CONV, 3)
    onward(OUT_A, 0)
    arrive(sig_full.at[1 - s], sig_sem.at[1])
    for side in range(2):
        sig_role[side * tokens : (side + 1) * tokens] = jnp.dot(
            to_role_ref[...], sig_full[side], preferred_element_type=jnp.float32
        ).astype(jnp.bfloat16)
    for k in range(RING):
        from_sibling(CONV, k)
    step(PROJ_A, 1)
    norm_rows(0, 2)
    step(PROJ_B, 1)
    onward(OUT_B, 0)
    norm_rows(2, 1)
    step(OUT_A, 0)
    norm_rows(3, 2)
    step(PROJ_A, 2)
    norm_rows(5, 1)
    step(OUT_B, 0)
    step(PROJ_B, 2)
    norm_rows(6, 2)
    step(OUT_A, 1)
    step(PROJ_A, 3)
    step_x(1, 5)
    start_total()
    step(OUT_B, 1)
    step(PROJ_B, 3)
    for k in range(RING):
        from_sibling(PROJ_A, k)
        from_sibling(PROJ_B, k)

    def second():
        step(OUT_A, 2)
        step_x(2, 6)
        step(OUT_B, 2)

    def third():
        step(OUT_A, 3)
        step_x(3, 7)
        step(OUT_B, 3)

    heads(0, second)
    heads(1, third)
    heads(2, lambda: step_x(4))
    heads(3)
    for j in range(HEADS // 4):
        theirs = pl.ds(pl.multiple_of((1 - s) * half + j * pair, pair), pair)
        arrive(joined.at[:, theirs], swap_recv.at[j])
    slots = (0, 1, 5, 2, 6, 3, 7, 4)
    partner = {0: 0, 1: 5, 5: 1, 2: 6, 6: 2, 3: 7, 7: 3, 4: 4}
    for k in slots:
        from_sibling(OUT_A, partner[k])
        from_sibling(OUT_B, partner[k])
        arrive(place_x(shard_of(partner[k], 1 - core, -d), 1 - s), sibx_recv.at[partner[k]])
        add_chip(k, last=k == 4)
    for copy in sent:
        copy.wait_send()


def split_by_branch(signal, conv_weight, conv_bias, ln_gain, ln_bias, w_space, w_time, w_out):
    s = lax.axis_index("seq")
    _, channels, patches, samples = signal.shape
    width = w_out.shape[1]
    half = width // 2
    tokens = channels * patches
    shards = 2 * RING
    rows = jnp.stack([conv_bias, ln_gain, ln_bias])
    conv = jnp.concatenate([conv_weight, jnp.pad(rows, ((0, 13), (0, 0)))], axis=0)
    patch_of = np.arange(2 * channels) // channels
    mask_a = (patch_of[:, None] == patch_of[None]).astype(np.float32)
    channel_of = np.tile(np.arange(8 * patches) // patches, 2)
    mask_b = (channel_of[:, None] == channel_of[None]).astype(np.float32)
    dma = pltpu.SemaphoreType.DMA
    vmem = pl.BlockSpec(memory_space=pltpu.VMEM)
    anywhere = pl.BlockSpec(memory_space=pl.ANY)
    bf16 = jnp.bfloat16
    flops = 4 * tokens * (width * samples + half * 3 * half + width * width // 2)
    mixed = pl.pallas_call(
        functools.partial(night_kernel, channels, patches),
        out_shape=jax.ShapeDtypeStruct((tokens, width), bf16),
        in_specs=[vmem, anywhere, anywhere, anywhere, anywhere, vmem, vmem],
        out_specs=vmem,
        scratch_shapes=[
            pltpu.VMEM((2, tokens, samples), bf16),
            pltpu.VMEM((2 * tokens, samples), bf16),
            pltpu.VMEM((conv.shape[0], width), bf16),
            pltpu.VMEM((shards * w_space.shape[0], w_space.shape[1]), bf16),
            pltpu.VMEM((shards * w_out.shape[0], width), bf16),
            pltpu.VMEM((2 * tokens, half), bf16),
            pltpu.VMEM((2 * tokens, 6 * width // HEADS), bf16),
            pltpu.VMEM((2 * tokens, half), bf16),
            pltpu.VMEM((tokens, half), bf16),
            pltpu.VMEM((tokens, width), bf16),
            pltpu.VMEM((tokens, width), jnp.float32),
            pltpu.VMEM((tokens, tokens), bf16),
            pltpu.VMEM((tokens, tokens), bf16),
            dma((5, 8)), dma((5, 8)), dma((5, 8)), dma((5, 8)),
            dma((8,)), dma((8,)), dma((8,)), dma((8,)), dma((3,)), dma((2,)), dma((4,)), dma((4,)),
        ],
        compiler_params=pltpu.CompilerParams(
            collective_id=0, has_side_effects=True, vmem_limit_bytes=60 * 2**20
        ),
        cost_estimate=pl.CostEstimate(flops=flops, bytes_accessed=2**23, transcendentals=2**21),
    )(signal.transpose(0, 2, 1, 3).reshape(tokens, samples), conv, w_space, w_time, w_out, jnp.asarray(mask_a),
      jnp.asarray(mask_b))
    return mixed.reshape(1, patches, channels, width).transpose(0, 2, 1, 3)


def solution(mesh):
    in_specs = (
        P("fsdp", None, "seq", None),
        P(None, "fsdp"),
        P("fsdp"),
        P("fsdp"),
        P("fsdp"),
        P("fsdp", None),
        P("fsdp", None),
        P("fsdp", None),
    )
    out_specs = P("fsdp", None, "seq", None)
    whole_night = mesh.shape["seq"] == 2 and mesh.shape["fsdp"] == 2 * RING
    body = split_by_branch if whole_night else per_device
    return jax.shard_map(
        body, mesh=mesh, in_specs=in_specs, out_specs=out_specs, check_vma=False
    )
```

```python
import functools
import math

import jax
import jax.numpy as jnp
import numpy as np
from jax import lax
from jax.experimental import pallas as pl
from jax.experimental.pallas import tpu as pltpu
from jax.sharding import PartitionSpec as P

HEADS = 16
MESH = pl.DeviceIdType.MESH


def layer_norm(values, gain, shift):
    mean = jnp.mean(values, axis=-1, keepdims=True)
    centred = values - mean
    variance = jnp.mean(centred * centred, axis=-1, keepdims=True)
    return centred * lax.rsqrt(variance + 1e-05) * gain.astype(jnp.float32) + shift.astype(
        jnp.float32
    )


def attend(queries, keys_in, values_in):
    scale = 1.0 / math.sqrt(queries.shape[-1])
    scores = (
        jnp.einsum("bqhd,bkhd->bhqk", queries, keys_in, preferred_element_type=jnp.float32) * scale
    )
    highest = jnp.max(scores, axis=-1, keepdims=True)
    expo = jnp.exp(scores - highest)
    probs = (expo / jnp.sum(expo, axis=-1, keepdims=True)).astype(jnp.bfloat16)
    result = jnp.einsum("bhqk,bkhd->bqhd", probs, values_in, preferred_element_type=jnp.float32)
    return result.astype(jnp.bfloat16)


def project(features, weight):
    return jnp.dot(
        features,
        lax.all_gather(weight, "fsdp", axis=0, tiled=True),
        preferred_element_type=jnp.float32,
    )


def per_device(signal, conv_weight, conv_bias, ln_gain, ln_bias, w_space, w_time, w_out):
    kernel, bias_full, gain_full, shift_full = (
        lax.all_gather(conv_weight, "fsdp", axis=1, tiled=True),
        lax.all_gather(conv_bias, "fsdp", axis=0, tiled=True),
        lax.all_gather(ln_gain, "fsdp", axis=0, tiled=True),
        lax.all_gather(ln_bias, "fsdp", axis=0, tiled=True),
    )
    nights, channels, patch_count, samples = signal.shape
    model_width = kernel.shape[1]
    half_width = model_width // 2
    head_count = HEADS // 2
    head_size = half_width // head_count
    flat = signal.reshape(-1, samples)
    embed = (
        jnp.dot(flat, kernel, preferred_element_type=jnp.float32) + bias_full.astype(jnp.float32)
    ).astype(jnp.bfloat16)
    embed = lax.optimization_barrier(embed)
    normed = layer_norm(embed.astype(jnp.float32), gain_full, shift_full).astype(jnp.bfloat16)
    space_qkv = project(normed[:, :half_width], w_space).astype(jnp.bfloat16)
    space_qkv = space_qkv.reshape(channels, patch_count, 3, head_count, head_size).transpose(
        1, 0, 2, 3, 4
    )
    space_out = attend(space_qkv[:, :, 0], space_qkv[:, :, 1], space_qkv[:, :, 2])
    space_out = space_out.transpose(1, 0, 2, 3).reshape(-1, half_width)
    time_qkv = project(normed[:, half_width:], w_time).astype(jnp.bfloat16)
    time_qkv = time_qkv.reshape(channels, patch_count, 3, head_count, head_size)
    local_out = attend(
        lax.all_to_all(time_qkv[:, :, 0], "seq", split_axis=0, concat_axis=1, tiled=True),
        lax.all_to_all(time_qkv[:, :, 1], "seq", split_axis=0, concat_axis=1, tiled=True),
        lax.all_to_all(time_qkv[:, :, 2], "seq", split_axis=0, concat_axis=1, tiled=True),
    )
    time_out = lax.all_to_all(local_out, "seq", split_axis=1, concat_axis=0, tiled=True)
    joined = jnp.concatenate([space_out, time_out.reshape(-1, half_width)], axis=1)
    mixed = embed.astype(jnp.float32) + project(joined, w_out)
    return mixed.astype(jnp.bfloat16).reshape(nights, channels, patch_count, model_width)


RING = 8
CONV, PROJ_A, PROJ_B, OUT_A, OUT_B = range(5)


def shard_at(position, core):
    position = lax.rem(position + 2 * RING, RING)
    y = position // 4
    z = jnp.where(y == 0, position, 7 - position)
    return (z * 2 + y) * 2 + core


ROWS = 160


def night_kernel(
    channels, patches, sig_ref, conv_ref, space_ref, time_ref, out_ref, mask_a_ref, mask_b_ref,
    mixed_ref,
    sig_full, sig_role, conv_full, proj_full, out_full, normed, qkv, result, outgoing, joined, total,
    to_role_ref, to_own_ref,
    ring_send, ring_recv, sib_send, sib_recv, x_send, x_recv, sibx_send, sibx_recv, own_sem, sig_sem,
    swap_send, swap_recv,
):
    s = lax.axis_index("seq")
    f = lax.axis_index("fsdp")
    core = lax.rem(f, 2)
    chip = f // 2
    y = lax.rem(chip, 2)
    z = chip // 2
    r = jnp.where(y == 0, z, 7 - z)
    d = 1 - 2 * core
    ahead = {"seq": s, "fsdp": shard_at(r + d, core)}
    behind = {"seq": s, "fsdp": shard_at(r - d, core)}
    sibling = {"seq": s, "fsdp": f + d}
    across = {"seq": 1 - s, "fsdp": f}
    depth, width = out_ref.shape
    half = width // 2
    cols = conv_ref.shape[1]
    proj_depth = space_ref.shape[0]
    tokens, samples = sig_ref.shape
    quarter = depth // 4
    head_size = width // HEADS
    pair = 2 * head_size

    def place(kind, shard):
        if kind == CONV:
            return conv_full.at[:, pl.ds(pl.multiple_of(shard * cols, cols), cols)]
        if kind in (PROJ_A, PROJ_B):
            count = proj_depth // 2
            start = pl.multiple_of(shard * proj_depth + (kind - PROJ_A) * count, count)
            return proj_full.at[pl.ds(start, count)]
        count = 3 * depth // 8
        first = s * (depth - count) if kind == OUT_A else count - s * (2 * count - 5 * depth // 8)
        return out_full.at[pl.ds(pl.multiple_of(shard * depth + first, 16), count)]

    def place_x(shard, side):
        start = pl.multiple_of(shard * depth + side * 3 * quarter, quarter)
        return out_full.at[pl.ds(start, quarter)]

    def shard_of(k, c, direction):
        if k <= 4:
            return shard_at(r - k * direction, c)
        return shard_at(r + (k - 4) * direction, c)

    own_conv = pltpu.make_async_copy(conv_ref, place(CONV, f), own_sem.at[0])
    own_proj_rows = pl.ds(pl.multiple_of(f * proj_depth, proj_depth), proj_depth)
    own_proj_a = pltpu.make_async_copy(space_ref, proj_full.at[own_proj_rows], own_sem.at[1])
    own_proj_b = pltpu.make_async_copy(time_ref, proj_full.at[own_proj_rows], own_sem.at[1])
    own_rows = pl.ds(pl.multiple_of(f * depth, depth), depth)
    own_out = pltpu.make_async_copy(out_ref, out_full.at[own_rows], own_sem.at[2])
    own_conv.start()
    pl.when(s == 0)(own_proj_a.start)
    pl.when(s == 1)(own_proj_b.start)
    own_out.start()

    barrier = pltpu.get_barrier_semaphore()
    for other in (ahead, behind, sibling, across):
        pl.semaphore_signal(barrier, inc=1, device_id=other, device_id_type=MESH)
    pl.semaphore_wait(barrier, 4)

    sent = []

    def send(src, dst, send_sem, recv_sem, device):
        copy = pltpu.make_async_remote_copy(
            src_ref=src, dst_ref=dst, send_sem=send_sem, recv_sem=recv_sem,
            device_id=device, device_id_type=MESH,
        )
        copy.start()
        sent.append(copy)

    def arrive(dst, recv_sem):
        pltpu.make_async_remote_copy(
            src_ref=dst, dst_ref=dst, send_sem=recv_sem, recv_sem=recv_sem,
            device_id=sibling, device_id_type=MESH,
        ).wait_recv()

    def onward(kind, k):
        shard = shard_of(k, core, d)
        dst = place(kind, shard)
        if k < 4:
            send(dst, dst, ring_send.at[kind, k + 1], ring_recv.at[kind, k + 1], ahead)
        if k == 0 or 5 <= k < 7:
            nxt = 5 if k == 0 else k + 1
            send(dst, dst, ring_send.at[kind, nxt], ring_recv.at[kind, nxt], behind)
        if kind == OUT_A and k == 0:
            quart = place_x(shard, 1 - s)
            send(quart, quart, sibx_send.at[0], sibx_recv.at[0], sibling)
        elif kind == OUT_A:
            quart = place_x(shard, s)
            send(quart, quart, x_send.at[k], x_recv.at[k], across)
        send(dst, dst, sib_send.at[kind, k], sib_recv.at[kind, k], sibling)

    both = ((1, 5), (2, 6), (3, 7), (4,))

    def step(kind, at):
        for k in both[at]:
            arrive(place(kind, shard_of(k, core, d)), ring_recv.at[kind, k])
            onward(kind, k)

    def step_x(*slots):
        for k in slots:
            dst = place_x(shard_of(k, core, d), 1 - s)
            arrive(dst, x_recv.at[k])
            send(dst, dst, sibx_send.at[k], sibx_recv.at[k], sibling)

    def from_sibling(kind, k):
        arrive(place(kind, shard_of(k, 1 - core, -d)), sib_recv.at[kind, k])

    def set_orders():
        row = lax.broadcasted_iota(jnp.int32, (tokens, 1), 0)
        col = lax.broadcasted_iota(jnp.int32, (tokens, tokens), 1)
        source = lax.rem(row, patches) * channels + lax.div(row, patches)
        to_role_ref[...] = (jnp.where(s == 0, row, source) == col).astype(jnp.bfloat16)
        target = lax.rem(row, channels) * patches + lax.div(row, channels)
        to_own_ref[...] = (jnp.where(s == 0, row, target) == col).astype(jnp.bfloat16)

    def embed(x):
        e = jnp.dot(x, conv_full[:samples], preferred_element_type=jnp.float32)
        return (e + conv_full[samples : samples + 1].astype(jnp.float32)).astype(jnp.bfloat16)

    def norm_rows(first, count):
        @pl.loop(first, first + count)
        def _(i):
            rows = pl.ds(pl.multiple_of(i * ROWS, ROWS), ROWS)
            e = embed(sig_role[rows]).astype(jnp.float32)
            mean = jnp.mean(e, axis=-1, keepdims=True)
            centred = e - mean
            variance = jnp.mean(centred * centred, axis=-1, keepdims=True)
            inverse = lax.rsqrt(variance + 1e-05)

            def keep(lo):
                part = slice(lo, lo + half)
                gain = conv_full[samples + 1 : samples + 2, part].astype(jnp.float32)
                shift = conv_full[samples + 2 : samples + 3, part].astype(jnp.float32)
                normed[rows] = (centred[:, part] * inverse * gain + shift).astype(jnp.bfloat16)

            pl.when(s == 0)(lambda: keep(0))
            pl.when(s == 1)(lambda: keep(half))

    def start_total():
        @pl.loop(0, tokens // ROWS)
        def _(i):
            rows = pl.ds(pl.multiple_of(i * ROWS, ROWS), ROWS)
            total[rows] = embed(sig_ref[rows]).astype(jnp.float32)

    def attend_rows(q, k, v, allowed):
        scores = lax.dot_general(
            q, k, (((1,), (1,)), ((), ())), preferred_element_type=jnp.float32
        ) * (1.0 / math.sqrt(head_size))
        scores = jnp.where(allowed, scores, -jnp.inf)
        highest = jnp.max(scores, axis=-1, keepdims=True)
        expo = jnp.exp(scores - highest)
        inverse = 1.0 / jnp.sum(expo, axis=-1, keepdims=True)
        probs = (expo * inverse).astype(jnp.bfloat16)
        return jnp.dot(probs, v, preferred_element_type=jnp.float32).astype(jnp.bfloat16)

    def heads(j, between=lambda: None):
        @pl.loop(0, 2 * tokens // (2 * ROWS))
        def _(i):
            rows = pl.ds(pl.multiple_of(i * 2 * ROWS, 2 * ROWS), 2 * ROWS)
            for part in range(3):
                w = proj_full[:, part * half + j * pair : part * half + (j + 1) * pair]
                value = jnp.dot(normed[rows], w, preferred_element_type=jnp.float32)
                qkv[rows, part * pair : (part + 1) * pair] = value.astype(jnp.bfloat16)

        between()
        at = slice(j * pair, (j + 1) * pair)

        @pl.when(s == 0)
        def _():
            count = mask_a_ref.shape[0]

            @pl.loop(0, 2 * tokens // count, unroll=2)
            def _(g):
                rows = pl.ds(pl.multiple_of(g * count, count), count)
                allowed = mask_a_ref[...] > 0
                for h in range(2):
                    q, k, v = (
                        qkv[rows, part * pair + h * head_size : part * pair + (h + 1) * head_size]
                        for part in range(3)
                    )
                    to = j * pair + h * head_size
                    result[rows, to : to + head_size] = attend_rows(q, k, v, allowed)

        @pl.when(s == 1)
        def _():
            count = mask_b_ref.shape[0] // 2

            @pl.loop(0, tokens // count, unroll=2)
            def _(g):
                first = pl.ds(pl.multiple_of(g * count, 16), count)
                second = pl.ds(pl.multiple_of(tokens + g * count, 16), count)
                allowed = mask_b_ref[...] > 0
                for h in range(2):
                    q, k, v = (
                        jnp.concatenate(
                            [
                                qkv[rows, part * pair + h * head_size : part * pair + (h + 1) * head_size]
                                for rows in (first, second)
                            ],
                            axis=0,
                        )
                        for part in range(3)
                    )
                    to = j * pair + h * head_size
                    value = attend_rows(q, k, v, allowed)
                    result[first, to : to + head_size] = value[:count]
                    result[second, to : to + head_size] = value[count:]

        mine = pl.ds(pl.multiple_of(s * half + j * pair, pair), pair)

        def reorder(side):
            rows = pl.ds(pl.multiple_of(side * tokens, tokens), tokens)
            return jnp.dot(
                to_own_ref[...], result[rows, at], preferred_element_type=jnp.float32
            ).astype(jnp.bfloat16)

        outgoing[:, at] = reorder(1 - s)
        send(outgoing.at[:, at], joined.at[:, mine], swap_send.at[j], swap_recv.at[j], across)
        joined[:, mine] = reorder(s)

    def add_chip(k, last=False):
        at = pl.ds(pl.multiple_of((shard_of(k, core, d) // 2) * 2 * depth, 2 * depth), 2 * depth)

        @pl.loop(0, tokens // ROWS)
        def _(i):
            rows = pl.ds(pl.multiple_of(i * ROWS, ROWS), ROWS)
            value = total[rows] + jnp.dot(
                joined[rows, at], out_full[at, :], preferred_element_type=jnp.float32
            )
            if last:
                mixed_ref[rows] = value.astype(jnp.bfloat16)
            else:
                total[rows] = value

    send(sig_ref, sig_full.at[s], sig_sem.at[0], sig_sem.at[1], across)
    own_conv.wait()
    onward(CONV, 0)
    pl.when(s == 0)(own_proj_a.wait)
    pl.when(s == 1)(own_proj_b.wait)
    onward(PROJ_A, 0)
    onward(PROJ_B, 0)
    own_out.wait()
    set_orders()
    step(CONV, 0)
    step(CONV, 1)
    sig_full[s] = sig_ref[...]
    step(PROJ_A, 0)
    step(CONV, 2)
    step(PROJ_B, 0)
    step(CONV, 3)
    onward(OUT_A, 0)
    arrive(sig_full.at[1 - s], sig_sem.at[1])
    for side in range(2):
        sig_role[side * tokens : (side + 1) * tokens] = jnp.dot(
            to_role_ref[...], sig_full[side], preferred_element_type=jnp.float32
        ).astype(jnp.bfloat16)
    for k in range(RING):
        from_sibling(CONV, k)
    step(PROJ_A, 1)
    norm_rows(0, 2)
    step(PROJ_B, 1)
    onward(OUT_B, 0)
    norm_rows(2, 1)
    step(OUT_A, 0)
    norm_rows(3, 2)
    step(PROJ_A, 2)
    norm_rows(5, 1)
    step(OUT_B, 0)
    step(PROJ_B, 2)
    norm_rows(6, 2)
    step(OUT_A, 1)
    step(PROJ_A, 3)
    step_x(1, 5)
    start_total()
    step(OUT_B, 1)
    step(PROJ_B, 3)
    for k in range(RING):
        from_sibling(PROJ_A, k)
        from_sibling(PROJ_B, k)

    def second():
        step(OUT_A, 2)
        step_x(2, 6)
        step(OUT_B, 2)

    def third():
        step(OUT_A, 3)
        step_x(3, 7)
        step(OUT_B, 3)

    heads(0, second)
    heads(1, third)
    heads(2, lambda: step_x(4))
    heads(3)
    for j in range(HEADS // 4):
        theirs = pl.ds(pl.multiple_of((1 - s) * half + j * pair, pair), pair)
        arrive(joined.at[:, theirs], swap_recv.at[j])
    slots = (0, 1, 5, 2, 6, 3, 7, 4)
    partner = {0: 0, 1: 5, 5: 1, 2: 6, 6: 2, 3: 7, 7: 3, 4: 4}
    for k in slots:
        from_sibling(OUT_A, partner[k])
        from_sibling(OUT_B, partner[k])
        arrive(place_x(shard_of(partner[k], 1 - core, -d), 1 - s), sibx_recv.at[partner[k]])
        add_chip(k, last=k == 4)
    for copy in sent:
        copy.wait_send()


def split_by_branch(signal, conv_weight, conv_bias, ln_gain, ln_bias, w_space, w_time, w_out):
    s = lax.axis_index("seq")
    _, channels, patches, samples = signal.shape
    width = w_out.shape[1]
    half = width // 2
    tokens = channels * patches
    shards = 2 * RING
    rows = jnp.stack([conv_bias, ln_gain, ln_bias])
    conv = jnp.concatenate([conv_weight, jnp.pad(rows, ((0, 13), (0, 0)))], axis=0)
    patch_of = np.arange(2 * channels) // channels
    mask_a = (patch_of[:, None] == patch_of[None]).astype(np.float32)
    channel_of = np.tile(np.arange(8 * patches) // patches, 2)
    mask_b = (channel_of[:, None] == channel_of[None]).astype(np.float32)
    dma = pltpu.SemaphoreType.DMA
    vmem = pl.BlockSpec(memory_space=pltpu.VMEM)
    anywhere = pl.BlockSpec(memory_space=pl.ANY)
    bf16 = jnp.bfloat16
    flops = 4 * tokens * (width * samples + half * 3 * half + width * width // 2)
    mixed = pl.pallas_call(
        functools.partial(night_kernel, channels, patches),
        out_shape=jax.ShapeDtypeStruct((tokens, width), bf16),
        in_specs=[vmem, anywhere, anywhere, anywhere, anywhere, vmem, vmem],
        out_specs=vmem,
        scratch_shapes=[
            pltpu.VMEM((2, tokens, samples), bf16),
            pltpu.VMEM((2 * tokens, samples), bf16),
            pltpu.VMEM((conv.shape[0], width), bf16),
            pltpu.VMEM((shards * w_space.shape[0], w_space.shape[1]), bf16),
            pltpu.VMEM((shards * w_out.shape[0], width), bf16),
            pltpu.VMEM((2 * tokens, half), bf16),
            pltpu.VMEM((2 * tokens, 6 * width // HEADS), bf16),
            pltpu.VMEM((2 * tokens, half), bf16),
            pltpu.VMEM((tokens, half), bf16),
            pltpu.VMEM((tokens, width), bf16),
            pltpu.VMEM((tokens, width), jnp.float32),
            pltpu.VMEM((tokens, tokens), bf16),
            pltpu.VMEM((tokens, tokens), bf16),
            dma((5, 8)), dma((5, 8)), dma((5, 8)), dma((5, 8)),
            dma((8,)), dma((8,)), dma((8,)), dma((8,)), dma((3,)), dma((2,)), dma((4,)), dma((4,)),
        ],
        compiler_params=pltpu.CompilerParams(
            collective_id=0, has_side_effects=True, vmem_limit_bytes=60 * 2**20
        ),
        cost_estimate=pl.CostEstimate(flops=flops, bytes_accessed=2**23, transcendentals=2**21),
    )(signal.transpose(0, 2, 1, 3).reshape(tokens, samples), conv, w_space, w_time, w_out, jnp.asarray(mask_a),
      jnp.asarray(mask_b))
    return mixed.reshape(1, patches, channels, width).transpose(0, 2, 1, 3)


def solution(mesh):
    in_specs = (
        P("fsdp", None, "seq", None),
        P(None, "fsdp"),
        P("fsdp"),
        P("fsdp"),
        P("fsdp"),
        P("fsdp", None),
        P("fsdp", None),
        P("fsdp", None),
    )
    out_specs = P("fsdp", None, "seq", None)
    whole_night = mesh.shape["seq"] == 2 and mesh.shape["fsdp"] == 2 * RING
    body = split_by_branch if whole_night else per_device
    return jax.shard_map(
        body, mesh=mesh, in_specs=in_specs, out_specs=out_specs, check_vma=False
    )
```
